256 devices in a mesh: dp: 64 (over z, x, core), mp: 4 (over y).
Axes of the slice: x: 4, y: 4, z: 8, core: 2. Of those that a mesh axis runs over, the one named last changes fastest.
Arguments:
- feature_ids: int32 [65536, 8], P('dp'), may hold values from 0 to 4095
- context_ids: int32 [65536], P('dp'), may hold values from 0 to 511
- shown_positions: int32 [65536], P('dp'), may hold values from 0 to 63
- clicked_positions: int32 [65536], P('dp'), may hold values from 0 to 63
- clicks: int32 [65536], P('dp'), may hold values 0 or 1
- embed_table: bfloat16 [4096, 1024], P(None, 'mp'), may hold values from -2 to 2
- cross_weight: bfloat16 [1024, 1024], P('dp', 'mp'), may hold values from -0.1875 to 0.1875
- deep_weight: bfloat16 [1024, 1024], P('dp', 'mp'), may hold values from -0.1875 to 0.1875
- cross_bias: float32 [1024], P('mp'), may hold values from -3 to 3
- deep_bias: float32 [1024], P('mp'), may hold values from -3 to 3
- out_weight: float32 [1024], P('mp'), may hold values from -0.1875 to 0.1875
- shown_embed: float32 [64, 64], replicated, may hold values from -4 to 4
- click_embed: float32 [64, 64], replicated, may hold values from -4 to 4
- theta_relevant: float32 [512, 64], P('mp'), may hold values from -2 to 2
- theta_irrelevant: float32 [512, 64], P('mp'), may hold values from -2 to 2
Outputs:
- bias_hessians: float32 [2, 512, 64, 64], P(None, 'mp', 'dp')
- bias_gradients: float32 [2, 512, 64], P(None, 'mp', 'dp')
- cross_update: float32 [1024, 1024], P('dp', 'mp')
- deep_update: float32 [1024, 1024], P('dp', 'mp')
- cross_bias_update: float32 [1024], P('mp')
- deep_bias_update: float32 [1024], P('mp')
- out_weight_update: float32 [1024], P('mp')
The draws below stay inside these ranges and needn't reach their ends.
All inputs are finite; a program needn't handle non-finite values. No bound on the sum of `clicks` on one device may be relied on, other than what follows from the above.
Results may differ from the reference program's by a relative error of at most 0.0085.
Values may be sent and summed in bfloat16 or wider, within the bound.
No kernel may reach another device: no remote copies, remote signals or barrier semaphores. Data moves between devices by JAX's collectives and lax.ppermute only.
A program may use at most 64 MiB of HBM per device.

```python
import math
import jax
import jax.numpy as jnp
import numpy as np
from jax import lax

D = 1024
POS = 64
BF = 64
NFEAT = 8
VOCAB = 4096
ROWS = 1024
NCTX = 512
TOTAL = 65536


def plant(drawn, rng, low, largest):
    shape = drawn.shape
    place = [jax.random.randint(jax.random.fold_in(rng, axis), (), 0, shape[axis]) for axis in range(len(shape))]
    drawn = drawn.at[tuple(place)].set(low)
    longest = shape.index(max(shape))
    place[longest] = (place[longest] + 1) % shape[longest]
    return drawn.at[tuple(place)].set(largest)


def block_scale(stream_key, extent, pieces, least, top_value):
    level = 1.0
    for dim, parts in pieces:
        heights = jax.random.uniform(jax.random.fold_in(jax.random.fold_in(stream_key, 6), dim), (parts,), jnp.float32, least / len(pieces), top_value / len(pieces))
        level = level * jnp.repeat(jnp.exp(heights), extent[dim] // parts).reshape((-1,) + (1,) * (len(extent) - 1 - dim))
    return level


def rank_table(count, skew):
    weights = [(1 << 20) // math.isqrt(rank ** skew) + 1 for rank in range(1, count + 1)]
    spread = 1 + sum(weights) // (1 << 30)
    return np.cumsum(np.array([max(1, weight // spread) for weight in weights]))


def skewed_ids(stream_key, shape, amount, skew):
    listing = rank_table(amount, skew)
    ticket = jax.random.randint(jax.random.fold_in(stream_key, 1), shape, 0, int(listing[amount - 1]))
    rank = jnp.searchsorted(jnp.asarray(listing, jnp.int32), ticket, side="right")
    return jax.random.permutation(jax.random.fold_in(stream_key, 2), amount)[rank].astype(jnp.int32)


def bell_draw(stream_key, extent, deviation, reach, split=(), kind=jnp.bfloat16):
    array = deviation * jax.random.normal(stream_key, extent, jnp.float32)
    if split:
        array = array * block_scale(stream_key, extent, split, -0.22, 0.18)
    return jnp.clip(array, -reach, reach).astype(kind)


def setup_inputs(seed: int = 0) -> dict:
    key_of = jax.random.split(jax.random.key(seed), 16)
    feature_ids = plant(skewed_ids(key_of[0], (TOTAL, NFEAT), VOCAB, 2), jax.random.fold_in(key_of[0], 3), 0, VOCAB - 1).astype(jnp.int32)
    context_ids = plant(jax.random.randint(key_of[1], (TOTAL,), 0, NCTX), jax.random.fold_in(key_of[1], 1), 0, NCTX - 1).astype(jnp.int32)
    shown_positions = plant(jax.random.randint(key_of[2], (TOTAL,), 0, POS), jax.random.fold_in(key_of[2], 1), 0, POS - 1).astype(jnp.int32)
    clicked_positions = plant(jax.random.randint(key_of[3], (TOTAL,), 0, POS), jax.random.fold_in(key_of[3], 1), 0, POS - 1).astype(jnp.int32)
    clicks = plant((jax.random.randint(key_of[4], (TOTAL,), 0, 3) < 1).astype(jnp.int32), jax.random.fold_in(key_of[4], 1), 0, 1)
    embed_table = bell_draw(key_of[5], (VOCAB, D), NFEAT ** -0.5, 2.0, ((1, 4),))
    cross_weight = bell_draw(key_of[6], (D, D), D ** -0.5, 0.1875, ((0, 64), (1, 4)))
    deep_weight = bell_draw(key_of[7], (D, D), D ** -0.5, 0.1875, ((0, 64), (1, 4)))
    cross_bias = bell_draw(key_of[8], (D,), 0.5, 3.0, ((0, 4),), jnp.float32)
    deep_bias = bell_draw(key_of[9], (D,), 0.5, 3.0, ((0, 4),), jnp.float32)
    out_weight = bell_draw(key_of[10], (D,), D ** -0.5, 0.1875, ((0, 4),), jnp.float32)
    shown_embed = bell_draw(key_of[11], (POS, BF), 0.7, 4.0, (), jnp.float32)
    click_embed = bell_draw(key_of[12], (POS, BF), 0.7, 4.0, (), jnp.float32)
    theta_relevant = bell_draw(key_of[13], (NCTX, BF), 0.3, 2.0, ((0, 4),), jnp.float32)
    theta_irrelevant = bell_draw(key_of[14], (NCTX, BF), 0.3, 2.0, ((0, 4),), jnp.float32)
    return dict(feature_ids=feature_ids, context_ids=context_ids, shown_positions=shown_positions, clicked_positions=clicked_positions, clicks=clicks, embed_table=embed_table, cross_weight=cross_weight, deep_weight=deep_weight, cross_bias=cross_bias, deep_bias=deep_bias, out_weight=out_weight, shown_embed=shown_embed, click_embed=click_embed, theta_relevant=theta_relevant, theta_irrelevant=theta_irrelevant)


def silu_parts(pre_act):
    gating = jax.nn.sigmoid(pre_act)
    return (pre_act * gating, gating * (1.0 + pre_act * (1.0 - gating)))

def posterior_of(relevance, mu_rel, mu_irr, click_float):
    on_click = mu_rel * relevance / (mu_rel * relevance + mu_irr * (1.0 - relevance))
    no_click = (1.0 - mu_rel) * relevance / ((1.0 - mu_rel) * relevance + (1.0 - mu_irr) * (1.0 - relevance))
    return jnp.where(click_float > 0.5, on_click, no_click)

def reference(feature_ids, context_ids, shown_positions, clicked_positions, clicks, embed_table, cross_weight, deep_weight, cross_bias, deep_bias, out_weight, shown_embed, click_embed, theta_relevant, theta_irrelevant):
    summed = jnp.zeros((feature_ids.shape[0], embed_table.shape[1]), jnp.float32)
    for slot_index in range(NFEAT):
        summed = summed + jnp.take(embed_table, feature_ids[:, slot_index], axis=0).astype(jnp.float32)
    base_rows = summed.astype(jnp.bfloat16)
    base_float = base_rows.astype(jnp.float32)
    cross_pre = jnp.dot(base_rows, cross_weight, preferred_element_type=jnp.float32)
    crossed = (base_float * (cross_pre + cross_bias) + base_float).astype(jnp.bfloat16)
    deep_pre = jnp.dot(crossed, deep_weight, preferred_element_type=jnp.float32) + deep_bias
    activated, slope = silu_parts(deep_pre)
    hidden = activated.astype(jnp.bfloat16)
    score_sum = lax.optimization_barrier(jnp.sum(hidden.astype(jnp.float32) * out_weight, axis=1))
    relevance = jax.nn.sigmoid(score_sum)
    features = jnp.tanh(shown_embed[shown_positions] + click_embed[clicked_positions])
    mu_rel = jax.nn.sigmoid(lax.optimization_barrier(jnp.sum(theta_relevant[context_ids] * features, axis=1)))
    mu_irr = jax.nn.sigmoid(lax.optimization_barrier(jnp.sum(theta_irrelevant[context_ids] * features, axis=1)))
    click_float = clicks.astype(jnp.float32)
    posterior = posterior_of(relevance, mu_rel, mu_irr, click_float)
    weights = jnp.stack([posterior * mu_rel * (1.0 - mu_rel), (1.0 - posterior) * mu_irr * (1.0 - mu_irr), posterior * (click_float - mu_rel), (1.0 - posterior) * (click_float - mu_irr)], axis=1)

    def add_block(running, row_block):
        ctx_block, feat_block, weight_block = row_block
        outer_prod = (feat_block[:, :, None] * feat_block[:, None, :]).reshape(feat_block.shape[0], -1)
        hess_new = jnp.stack([jax.ops.segment_sum(weight_block[:, 0:1] * outer_prod, ctx_block, NCTX), jax.ops.segment_sum(weight_block[:, 1:2] * outer_prod, ctx_block, NCTX)])
        grad_new = jnp.stack([jax.ops.segment_sum(weight_block[:, 2:3] * feat_block, ctx_block, NCTX), jax.ops.segment_sum(weight_block[:, 3:4] * feat_block, ctx_block, NCTX)])
        return ((running[0] + hess_new, running[1] + grad_new), None)
    start_stats = (jnp.zeros((2, NCTX, BF * BF), jnp.float32), jnp.zeros((2, NCTX, BF), jnp.float32))
    blocks = (context_ids.reshape(-1, ROWS), features.reshape(-1, ROWS, BF), weights.reshape(-1, ROWS, 4))
    (hess_all, grad_all), unused = lax.scan(add_block, start_stats, blocks)
    bias_hessians = hess_all.reshape(2, NCTX, BF, BF)
    score_grad = relevance - posterior
    pre_grad = score_grad[:, None] * out_weight[None, :] * slope
    pre_grad_b = pre_grad.astype(jnp.bfloat16)
    deep_grad = jnp.dot(crossed.T, pre_grad_b, preferred_element_type=jnp.float32)
    deep_bias_grad = lax.optimization_barrier(jnp.sum(pre_grad, axis=0))
    out_grad = lax.optimization_barrier(jnp.sum(score_grad[:, None] * hidden.astype(jnp.float32), axis=0))
    crossed_grad = jnp.dot(pre_grad_b, deep_weight.T, preferred_element_type=jnp.float32)
    cross_pre_grad = crossed_grad * base_float
    cross_pre_b = cross_pre_grad.astype(jnp.bfloat16)
    cross_grad = jnp.dot(base_rows.T, cross_pre_b, preferred_element_type=jnp.float32)
    cross_bias_grad = lax.optimization_barrier(jnp.sum(cross_pre_grad, axis=0))
    squares = jnp.sum(cross_grad * cross_grad) + jnp.sum(deep_grad * deep_grad) + jnp.sum(cross_bias_grad * cross_bias_grad) + jnp.sum(deep_bias_grad * deep_bias_grad) + jnp.sum(out_grad * out_grad)
    norm_scale = 1.0 / jnp.sqrt(squares / (2 * D * D + 3 * D) + 1e-06)
    return (bias_hessians, grad_all, cross_grad * norm_scale, deep_grad * norm_scale, cross_bias_grad * norm_scale, deep_bias_grad * norm_scale, out_grad * norm_scale)
```

```python
import jax
import jax.numpy as jnp
import numpy as np
from jax import lax
from jax.experimental import pallas as pl
from jax.experimental.pallas import tpu as pltpu
from jax.sharding import Mesh, PartitionSpec as P

DP = ("z", "x", "c")
BF16 = jnp.bfloat16
F32 = jnp.float32


def posterior_of(relevance, mu_rel, mu_irr, click_float):
    on_click = mu_rel * relevance / (mu_rel * relevance + mu_irr * (1.0 - relevance))
    no_click = (
        (1.0 - mu_rel)
        * relevance
        / ((1.0 - mu_rel) * relevance + (1.0 - mu_irr) * (1.0 - relevance))
    )
    return jnp.where(click_float > 0.5, on_click, no_click)


def table_lookup(indices, table):
    onehot_rows = (indices[:, None] == jnp.arange(table.shape[0])[None, :]).astype(F32)
    return jnp.dot(onehot_rows, table, precision=lax.Precision.HIGHEST)


def embed_kernel(ids_ref, table_ref, out_ref, wide_ref):
    rows, slots = ids_ref.shape
    vocab, width = table_ref.shape
    lanes = 256
    tile = 256
    ids = ids_ref[...]
    for s in range(slots):
        wide_ref[s] = jnp.broadcast_to(ids[:, s : s + 1], (rows, lanes)).astype(jnp.int16)
    lane = lax.broadcasted_iota(jnp.int32, (tile, lanes), 1)

    def body(r, carry):
        first = pl.multiple_of(r * tile, tile)
        total = jnp.zeros((tile, width), F32)
        for k in range(vocab // lanes):
            names = (lane + k * lanes).astype(jnp.int16)
            counts = jnp.zeros((tile, lanes), BF16)
            for s in range(slots):
                hit = wide_ref[s, pl.ds(first, tile), :] == names
                counts = counts + jnp.where(hit, jnp.ones((), BF16), jnp.zeros((), BF16))
            total = total + jnp.dot(
                counts, table_ref[k * lanes : (k + 1) * lanes, :], preferred_element_type=F32
            )
        out_ref[pl.ds(first, tile), :] = total.astype(BF16)
        return carry

    lax.fori_loop(0, rows // tile, body, 0)


def embed(ids, table):
    rows = ids.shape[0]
    return pl.pallas_call(
        embed_kernel,
        out_shape=jax.ShapeDtypeStruct((rows, table.shape[1]), BF16),
        in_specs=[pl.BlockSpec(memory_space=pltpu.VMEM)] * 2,
        out_specs=pl.BlockSpec(memory_space=pltpu.VMEM),
        scratch_shapes=[pltpu.VMEM((ids.shape[1], rows, 256), jnp.int16)],
        compiler_params=pltpu.CompilerParams(vmem_limit_bytes=40 * 2**20),
    )(ids, table)


def swap(value):
    return lax.ppermute(value, "c", [(0, 1), (1, 0)])


def gather(value, axes, count):
    wide = jnp.broadcast_to(value[None], (count,) + value.shape)
    return lax.all_to_all(wide, axes, 0, 0, tiled=True)


def shards(
    feature_ids,
    context_ids,
    shown_positions,
    clicked_positions,
    clicks,
    embed_table,
    cross_weight,
    deep_weight,
    cross_bias,
    deep_bias,
    out_weight,
    shown_embed,
    click_embed,
    theta_relevant,
    theta_irrelevant,
):
    n_z, n_x, n_mp = lax.axis_size("z"), lax.axis_size("x"), lax.axis_size("mp")
    n_zx = n_z * n_x
    n_dp = 2 * n_zx
    row_count = context_ids.shape[0]
    part = row_count // n_mp
    depth, width = cross_weight.shape
    full = n_mp * width
    core = lax.axis_index("c")
    mine = lax.axis_index("mp")

    with jax.named_scope("weights_dp"):
        both = jnp.stack([cross_weight, deep_weight])
        held = gather(both, ("z", "x"), n_zx)
        other = swap(held)
        cores = jnp.where(core == 0, jnp.stack([held, other], 1), jnp.stack([other, held], 1))
        cross_col = cores[:, :, 0].reshape(full, width)
    with jax.named_scope("deep_weight_mp"):
        deep_all = gather(held[:, 1], "mp", n_mp)
        deep_other = swap(deep_all)
        deep_cores = jnp.where(
            core == 0, jnp.stack([deep_all, deep_other], 2), jnp.stack([deep_other, deep_all], 2)
        )
        deep_full = deep_cores.transpose(1, 2, 3, 0, 4).reshape(full, full)
    with jax.named_scope("vectors_mp"):
        vectors = gather(jnp.stack([deep_bias, out_weight]), "mp", n_mp)
        deep_bias_full = vectors[:, 0].reshape(full)
        out_full = vectors[:, 1].reshape(full)

    with jax.named_scope("embed"):
        base_rows = embed(feature_ids, embed_table)
        base_float = base_rows.astype(F32)
    with jax.named_scope("base_mp"):
        base_full = gather(base_rows, "mp", n_mp).transpose(1, 0, 2).reshape(row_count, full)

    with jax.named_scope("click_models"):
        ctx_count = theta_relevant.shape[0]
        local_ctx = context_ids - mine * ctx_count
        select = local_ctx[:, None] == jnp.arange(ctx_count)[None, :]
        selector = select.astype(F32)
        owned = (local_ctx >= 0) & (local_ctx < ctx_count)
        features = jnp.tanh(
            table_lookup(shown_positions, shown_embed)
            + table_lookup(clicked_positions, click_embed)
        )
        rel_rows = jnp.dot(selector, theta_relevant, precision=lax.Precision.HIGHEST)
        irr_rows = jnp.dot(selector, theta_irrelevant, precision=lax.Precision.HIGHEST)
        mu_rel = jax.nn.sigmoid(jnp.sum(rel_rows * features, axis=1))
        mu_irr = jax.nn.sigmoid(jnp.sum(irr_rows * features, axis=1))
        click_float = clicks.astype(F32)
        features_t = features.T
        sent = jnp.where(owned[None, :], jnp.stack([mu_rel, mu_irr]), 0.0)
        sent = sent.reshape(2, n_mp, part).transpose(1, 0, 2)
        mu_mine = jnp.sum(lax.all_to_all(sent, "mp", 0, 0, tiled=True), axis=0)
        click_mine = lax.dynamic_slice(click_float, (mine * part,), (part,))

    with jax.named_scope("cross"):
        cross_pre = jnp.dot(base_full, cross_col, preferred_element_type=F32)
        crossed = (base_float * (cross_pre + cross_bias) + base_float).astype(BF16)
    with jax.named_scope("crossed_mp"):
        crossed_mine = lax.all_to_all(crossed.reshape(n_mp, part, width), "mp", 0, 0, tiled=True)
        crossed_mine = crossed_mine.transpose(1, 0, 2).reshape(part, full)
    with jax.named_scope("deep"):
        deep_pre = jnp.dot(crossed_mine, deep_full, preferred_element_type=F32) + deep_bias_full
        gating = jax.nn.sigmoid(deep_pre)
        hidden = (deep_pre * gating).astype(BF16).astype(F32)
        slope = gating * (1.0 + deep_pre * (1.0 - gating))
        score = jnp.sum(hidden * out_full, axis=1)
        rel_mine = jax.nn.sigmoid(score)
        post_mine = posterior_of(rel_mine, mu_mine[0], mu_mine[1], click_mine)
        score_grad = rel_mine - post_mine
        pre_grad = score_grad[:, None] * out_full[None, :] * slope
        pre_grad_b = pre_grad.astype(BF16)
        deep_bias_part = jnp.sum(pre_grad, axis=0)
        out_part = jnp.sum(score_grad[:, None] * hidden, axis=0)
    with jax.named_scope("crossed_grad"):
        crossed_grad = lax.dot_general(
            pre_grad_b, deep_full, (((1,), (1,)), ((), ())), preferred_element_type=F32
        ).astype(BF16)
        back = crossed_grad.reshape(part, n_mp, width).transpose(1, 0, 2)
        extra = jnp.stack([deep_bias_part, out_part]).reshape(2, n_mp, width).transpose(1, 0, 2)
        extra_hi = extra.astype(BF16)
        extra_lo = (extra - extra_hi.astype(F32)).astype(BF16)
        pad = jnp.zeros((n_mp, 4, width), BF16)
        back = lax.all_to_all(
            jnp.concatenate([back, extra_hi, extra_lo, pad], axis=1), "mp", 0, 0, tiled=True
        )
        crossed_back = back[:, :part].reshape(row_count, width).astype(F32)
        extra_sum = jnp.sum(
            back[:, part : part + 2].astype(F32) + back[:, part + 2 : part + 4].astype(F32), axis=0
        )
    with jax.named_scope("deep_grad"):
        deep_part = lax.dot_general(
            crossed_mine, pre_grad_b, (((0,), (0,)), ((), ())), preferred_element_type=F32
        )
        deep_part = deep_part.reshape(n_zx, 2, depth, full)
        deep_keep = jnp.where(core == 0, deep_part[:, 0], deep_part[:, 1])
        deep_send = jnp.where(core == 0, deep_part[:, 1], deep_part[:, 0]).astype(BF16)
        deep_pair = (deep_keep + swap(deep_send).astype(F32)).astype(BF16)
        deep_pair = deep_pair.reshape(n_z, n_x, depth, n_mp, width).transpose(1, 3, 0, 2, 4)
        deep_pair = deep_pair.reshape(n_x * n_mp, n_z, depth, width)
        deep_xm = lax.all_to_all(deep_pair, ("x", "mp"), 0, 0, tiled=True)
        deep_xm = jnp.sum(deep_xm.astype(F32), axis=0).astype(BF16)
        deep_z = lax.all_to_all(deep_xm, "z", 0, 0, tiled=True)
        deep_shard = jnp.sum(deep_z.astype(F32), axis=0)

    with jax.named_scope("cross_grad"):
        cross_pre_grad = crossed_back * base_float
        cross_pre_b = cross_pre_grad.astype(BF16)
        cross_part = lax.dot_general(
            base_full, cross_pre_b, (((0,), (0,)), ((), ())), preferred_element_type=F32
        )
        vec_part = jnp.concatenate([jnp.sum(cross_pre_grad, axis=0)[None], extra_sum])
        message = jnp.concatenate(
            [
                cross_part.astype(BF16).reshape(n_dp, depth, width),
                jnp.broadcast_to(vec_part.astype(BF16)[None], (n_dp, 3, width)),
                jnp.zeros((n_dp, 5, width), BF16),
            ],
            axis=1,
        )
        got = lax.all_to_all(message, DP, 0, 0, tiled=True)
        got_sum = jnp.sum(got.astype(F32), axis=0)
        cross_shard = got_sum[:depth]
        vec_sum = got_sum[depth : depth + 3]

    with jax.named_scope("norm"):
        local_squares = (
            jnp.sum(cross_shard * cross_shard)
            + jnp.sum(deep_shard * deep_shard)
            + jnp.where(lax.axis_index(DP) == 0, jnp.sum(vec_sum * vec_sum), 0.0)
        )
        squares = jnp.broadcast_to(local_squares, (n_dp, 128))
        squares = jnp.sum(lax.all_to_all(squares, DP, 0, 0, tiled=True), axis=0)
        squares = jnp.broadcast_to(squares[None], (n_mp, 128))
        squares = jnp.sum(lax.all_to_all(squares, "mp", 0, 0, tiled=True), axis=0)[0]
        norm_scale = 1.0 / jnp.sqrt(squares / (2 * full * full + 3 * full) + 1e-06)

    with jax.named_scope("relevance_mp"):
        relevance = gather(rel_mine, "mp", n_mp).reshape(row_count)
    with jax.named_scope("stats"):
        posterior = posterior_of(relevance, mu_rel, mu_irr, click_float)
        hess_w = jnp.concatenate(
            [
                selector * (posterior * mu_rel * (1.0 - mu_rel))[:, None],
                selector * ((1.0 - posterior) * mu_irr * (1.0 - mu_irr))[:, None],
            ],
            axis=1,
        ).astype(BF16)
        grad_w = jnp.concatenate(
            [
                selector * (posterior * (click_float - mu_rel))[:, None],
                selector * ((1.0 - posterior) * (click_float - mu_irr))[:, None],
            ],
            axis=1,
        )
        feats = features.shape[1]
        outer = (features_t[:, None, :] * features_t[None, :, :]).astype(BF16)
        hess_part = jnp.dot(
            outer.reshape(feats * feats, row_count), hess_w, preferred_element_type=F32
        ).reshape(feats, feats, 2 * ctx_count)
        grad_part = jnp.dot(features_t, grad_w, precision=lax.Precision.HIGHEST)
        stats = jnp.concatenate(
            [hess_part, grad_part[:, None, :], jnp.zeros((feats, 7, 2 * ctx_count), F32)], axis=1
        )
        stats = stats.reshape(n_zx, 2, feats + 8, 2 * ctx_count)
        stats_keep = jnp.where(core == 0, stats[:, 0], stats[:, 1])
        stats_send = jnp.where(core == 0, stats[:, 1], stats[:, 0]).astype(BF16)
        stats_pair = (stats_keep + swap(stats_send).astype(F32)).astype(BF16)
        stats_zx = lax.all_to_all(stats_pair, ("z", "x"), 0, 0, tiled=True)
        stats_sum = jnp.sum(stats_zx.astype(F32), axis=0)
        hess_out = stats_sum[:feats].T.reshape(2, ctx_count, 1, feats)
        stat_grad_out = stats_sum[feats].reshape(2, ctx_count, 1)

    return (
        hess_out,
        stat_grad_out,
        cross_shard * norm_scale,
        deep_shard * norm_scale,
        vec_sum[0] * norm_scale,
        vec_sum[1] * norm_scale,
        vec_sum[2] * norm_scale,
    )


def solution(mesh):
    devices = np.asarray(mesh.devices).reshape(8, 4, 2, 4)
    fine = Mesh(devices, ("z", "x", "c", "mp"))
    return jax.shard_map(
        shards,
        mesh=fine,
        in_specs=(
            P(DP, None),
            P(DP),
            P(DP),
            P(DP),
            P(DP),
            P(None, "mp"),
            P(DP, "mp"),
            P(DP, "mp"),
            P("mp"),
            P("mp"),
            P("mp"),
            P(),
            P(),
            P("mp", None),
            P("mp", None),
        ),
        out_specs=(
            P(None, "mp", DP, None),
            P(None, "mp", DP),
            P(DP, "mp"),
            P(DP, "mp"),
            P("mp"),
            P("mp"),
            P("mp"),
        ),
        check_vma=False,
    )
```

```python
import jax
import jax.numpy as jnp
import numpy as np
from jax import lax
from jax.experimental import pallas as pl
from jax.experimental.pallas import tpu as pltpu
from jax.sharding import Mesh, PartitionSpec as P

DP = ("z", "x", "c")
BF16 = jnp.bfloat16
F32 = jnp.float32


def posterior_of(relevance, mu_rel, mu_irr, click_float):
    on_click = mu_rel * relevance / (mu_rel * relevance + mu_irr * (1.0 - relevance))
    no_click = (
        (1.0 - mu_rel)
        * relevance
        / ((1.0 - mu_rel) * relevance + (1.0 - mu_irr) * (1.0 - relevance))
    )
    return jnp.where(click_float > 0.5, on_click, no_click)


def table_lookup(indices, table):
    onehot_rows = (indices[:, None] == jnp.arange(table.shape[0])[None, :]).astype(F32)
    return jnp.dot(onehot_rows, table, precision=lax.Precision.HIGHEST)


def embed_kernel(ids_ref, table_ref, out_ref, wide_ref):
    rows, slots = ids_ref.shape
    vocab, width = table_ref.shape
    lanes = 256
    tile = 256
    ids = ids_ref[...]
    for s in range(slots):
        wide_ref[s] = jnp.broadcast_to(ids[:, s : s + 1], (rows, lanes)).astype(jnp.int16)
    lane = lax.broadcasted_iota(jnp.int32, (tile, lanes), 1)

    def body(r, carry):
        first = pl.multiple_of(r * tile, tile)
        total = jnp.zeros((tile, width), F32)
        for k in range(vocab // lanes):
            names = (lane + k * lanes).astype(jnp.int16)
            counts = jnp.zeros((tile, lanes), BF16)
            for s in range(slots):
                hit = wide_ref[s, pl.ds(first, tile), :] == names
                counts = counts + jnp.where(hit, jnp.ones((), BF16), jnp.zeros((), BF16))
            total = total + jnp.dot(
                counts, table_ref[k * lanes : (k + 1) * lanes, :], preferred_element_type=F32
            )
        out_ref[pl.ds(first, tile), :] = total.astype(BF16)
        return carry

    lax.fori_loop(0, rows // tile, body, 0)


def embed(ids, table):
    rows = ids.shape[0]
    return pl.pallas_call(
        embed_kernel,
        out_shape=jax.ShapeDtypeStruct((rows, table.shape[1]), BF16),
        in_specs=[pl.BlockSpec(memory_space=pltpu.VMEM)] * 2,
        out_specs=pl.BlockSpec(memory_space=pltpu.VMEM),
        scratch_shapes=[pltpu.VMEM((ids.shape[1], rows, 256), jnp.int16)],
        compiler_params=pltpu.CompilerParams(vmem_limit_bytes=40 * 2**20),
    )(ids, table)


def stats_kernel(core_ref, feats_ref, weights_ref, grads_ref, keep_ref, send_ref):
    feats = feats_ref.shape[0]
    group = 4
    core = core_ref[0]
    head = lax.broadcasted_iota(jnp.int32, (16, grads_ref.shape[1]), 0) == 0
    for out_ref, side in ((keep_ref, core), (send_ref, 1 - core)):

        def body(g, carry, out_ref=out_ref, side=side):
            features = feats_ref[...]
            places = [2 * (group * g + q) + side for q in range(group)]
            outer = jnp.concatenate(
                [(features * feats_ref[pl.ds(i, 1), :]).astype(BF16) for i in places]
            )
            sums = jnp.dot(outer, weights_ref[...], preferred_element_type=F32)
            for q in range(group):
                out_ref[group * g + q, 0:feats, :] = sums[q * feats : (q + 1) * feats].astype(BF16)
                row = jnp.where(head, grads_ref[pl.ds(places[q], 1), :], 0.0)
                out_ref[group * g + q, feats : feats + 16, :] = row.astype(BF16)
            return carry

        lax.fori_loop(0, feats // (2 * group), body, 0)


def stats_blocks(core, features_t, hess_w, grad_part):
    feats, columns = grad_part.shape
    shape = jax.ShapeDtypeStruct((feats // 2, feats + 16, columns), BF16)
    vmem = pl.BlockSpec(memory_space=pltpu.VMEM)
    return pl.pallas_call(
        stats_kernel,
        out_shape=(shape, shape),
        in_specs=[pl.BlockSpec(memory_space=pltpu.SMEM), vmem, vmem, vmem],
        out_specs=(vmem, vmem),
        compiler_params=pltpu.CompilerParams(vmem_limit_bytes=32 * 2**20),
        cost_estimate=pl.CostEstimate(flops=1000, transcendentals=0, bytes_accessed=1000),
    )(core.reshape(1).astype(jnp.int32), features_t, hess_w, grad_part)


def swap(value):
    return lax.ppermute(value, "c", [(0, 1), (1, 0)])


def gather(value, axes, count):
    wide = jnp.broadcast_to(value[None], (count,) + value.shape)
    return lax.all_to_all(wide, axes, 0, 0, tiled=True)


def shift(value, axis, count, ahead):
    return lax.ppermute(value, axis, [(i, (i + ahead) % count) for i in range(count)])


def gather_ahead(value, axis, count):
    return [value] + [shift(value, axis, count, count - t) for t in range(1, count)]


def scatter_ahead(parts, axis):
    count = len(parts)
    total = parts[0].astype(F32)
    for arrived in [shift(parts[t], axis, count, t) for t in range(1, count)]:
        total = total + arrived.astype(F32)
    return total


def to_absolute(blocks, mine):
    count = blocks.shape[0]
    return lax.dynamic_slice_in_dim(
        jnp.concatenate([blocks, blocks]), (count - mine) % count, count, 0
    )


def to_ahead(blocks, mine):
    return lax.dynamic_slice_in_dim(jnp.concatenate([blocks, blocks]), mine, blocks.shape[0], 0)


def block_ahead(blocks, mine, t, dim=0):
    count = blocks.shape[dim]
    return lax.dynamic_index_in_dim(blocks, (mine + t) % count, dim, keepdims=False)


def after(value, *earlier):
    return lax.optimization_barrier((value,) + earlier)[0]


def split3(value):
    high = lax.reduce_precision(value, 8, 7)
    rest = value - high
    middle = lax.reduce_precision(rest, 8, 7)
    return jnp.concatenate([high, middle, rest - middle], axis=-2).astype(BF16)


def join3(value):
    high, middle, low = jnp.split(value.astype(F32), 3, axis=-2)
    return high + (middle + low)


def by_core(core, even, odd):
    return jnp.where(core == 0, even, odd)


def shards(
    feature_ids,
    context_ids,
    shown_positions,
    clicked_positions,
    clicks,
    embed_table,
    cross_weight,
    deep_weight,
    cross_bias,
    deep_bias,
    out_weight,
    shown_embed,
    click_embed,
    theta_relevant,
    theta_irrelevant,
):
    n_z, n_x, n_mp = lax.axis_size("z"), lax.axis_size("x"), lax.axis_size("mp")
    n_zx = n_z * n_x
    n_dp = 2 * n_zx
    row_count = context_ids.shape[0]
    part = row_count // n_mp
    depth, width = cross_weight.shape
    full = n_mp * width
    half = full // 2
    core = lax.axis_index("c")
    mine = lax.axis_index("mp")

    my_x = lax.axis_index("x")

    with jax.named_scope("weights_dp"):
        held = gather(jnp.concatenate([cross_weight, deep_weight]), DP, n_dp)
        cross_col = held[:, :depth].reshape(full, width)
        deep_col = held[:, depth:].reshape(full, width)
    with jax.named_scope("embed"):
        base_rows = embed(feature_ids, embed_table)
        base_float = base_rows.astype(F32)
    with jax.named_scope("base_mp"):
        base = gather_ahead(base_rows, "mp", n_mp)

    with jax.named_scope("click_models"):
        context_ids = after(context_ids, held)
        shown_positions = after(shown_positions, held)
        clicked_positions = after(clicked_positions, held)
        ctx_count = theta_relevant.shape[0]
        local_ctx = context_ids - mine * ctx_count
        select = local_ctx[:, None] == jnp.arange(ctx_count)[None, :]
        selector = select.astype(F32)
        owned = (local_ctx >= 0) & (local_ctx < ctx_count)
        features = jnp.tanh(
            table_lookup(shown_positions, shown_embed)
            + table_lookup(clicked_positions, click_embed)
        )
        rel_rows = jnp.dot(selector, theta_relevant, precision=lax.Precision.HIGHEST)
        irr_rows = jnp.dot(selector, theta_irrelevant, precision=lax.Precision.HIGHEST)
        mu_rel = jax.nn.sigmoid(jnp.sum(rel_rows * features, axis=1))
        mu_irr = jax.nn.sigmoid(jnp.sum(irr_rows * features, axis=1))
        click_float = clicks.astype(F32)
        features_t = features.T
        click_mine = lax.dynamic_slice(click_float, (mine * part,), (part,))
    with jax.named_scope("vectors"):
        sent = jnp.where(owned[None, :], jnp.stack([mu_rel, mu_irr]), 0.0)
        sent = sent.reshape(2, n_mp, part).transpose(1, 0, 2)
        vectors = jnp.broadcast_to(jnp.stack([deep_bias, out_weight])[None], (n_mp, 2, width))
        vectors = split3(jnp.concatenate([sent, vectors], axis=1))
        vectors = jnp.concatenate([vectors, jnp.zeros((n_mp, 4, width), BF16)], axis=1)
        vectors = lax.optimization_barrier(vectors)

    with jax.named_scope("deep_weight_mp"):
        deep_half = lax.dynamic_slice(deep_col, (core * half, 0), (half, width))
        deep_half = gather_ahead(deep_half, "mp", n_mp)

    with jax.named_scope("cross"):
        cross_pre = cross_bias
        for t in range(n_mp):
            rows_t = lax.dynamic_slice(
                cross_col, (((mine + t) % n_mp) * width, 0), (width, width)
            )
            cross_pre = cross_pre + jnp.dot(base[t], rows_t, preferred_element_type=F32)
        crossed = (base_float * cross_pre + base_float).astype(BF16)
    with jax.named_scope("crossed_mp"):
        arrived = jnp.concatenate([crossed.reshape(n_mp, part, width), vectors], axis=1)
        arrived = lax.all_to_all(arrived, "mp", 0, 0, tiled=True)
        crossed_mine = arrived[:, :part].transpose(1, 0, 2).reshape(part, full)
        vectors = join3(arrived[:, part : part + 12])
        mu_mine = jnp.sum(vectors[:, :2], axis=0)
        vectors = to_ahead(vectors, mine)
        deep_bias_full = vectors[:, 2].reshape(full)
        out_full = vectors[:, 3].reshape(full)
    with jax.named_scope("deep_weight_core"):
        deep_half = lax.optimization_barrier((crossed, *deep_half))[1:]
        deep_half = jnp.concatenate(deep_half, axis=1)
        deep_other = swap(deep_half)
        deep_top = by_core(core, deep_half, deep_other)
        deep_low = by_core(core, deep_other, deep_half)
    with jax.named_scope("deep"):
        deep_pre = (
            jnp.dot(crossed_mine[:, :half], deep_top, preferred_element_type=F32)
            + jnp.dot(crossed_mine[:, half:], deep_low, preferred_element_type=F32)
            + deep_bias_full
        )
        gating = jax.nn.sigmoid(deep_pre)
        hidden = (deep_pre * gating).astype(BF16).astype(F32)
        slope = gating * (1.0 + deep_pre * (1.0 - gating))
        score = jnp.sum(hidden * out_full, axis=1)
        rel_mine = jax.nn.sigmoid(score)
        post_mine = posterior_of(rel_mine, mu_mine[0], mu_mine[1], click_mine)
        score_grad = rel_mine - post_mine
        pre_grad = score_grad[:, None] * out_full[None, :] * slope
        pre_grad_b = pre_grad.astype(BF16)
        deep_bias_part = jnp.sum(pre_grad, axis=0)
        out_part = jnp.sum(score_grad[:, None] * hidden, axis=0)
    with jax.named_scope("crossed_grad"):
        back = []
        for k in range(n_mp):
            rows = deep_top if k * width < half else deep_low
            first = (k * width) % half
            back.append(
                lax.dot_general(
                    pre_grad_b,
                    rows[first : first + width],
                    (((1,), (1,)), ((), ())),
                    preferred_element_type=F32,
                ).astype(BF16)
            )
        back = jnp.stack(back)
        extra = jnp.stack([deep_bias_part, out_part]).reshape(2, n_mp, width).transpose(1, 0, 2)
        extra = to_absolute(extra, mine)
        tail = jnp.concatenate([split3(extra), jnp.zeros((n_mp, 2, width), BF16)], axis=1)
        tail = lax.optimization_barrier(tail)
        back = jnp.concatenate([back, tail], axis=1)
        rel_sent = after(rel_mine, back)
        back = lax.all_to_all(back, "mp", 0, 0, tiled=True)
        crossed_back = back[:, :part].reshape(row_count, width).astype(F32)
        extra_sum = jnp.sum(join3(back[:, part : part + 6]), axis=0)
    with jax.named_scope("stats"):
        relevance = jnp.stack(gather_ahead(rel_sent, "mp", n_mp))
        relevance = to_absolute(relevance, mine).reshape(row_count)
        posterior = posterior_of(relevance, mu_rel, mu_irr, click_float)
        hess_w = jnp.concatenate(
            [
                selector * (posterior * mu_rel * (1.0 - mu_rel))[:, None],
                selector * ((1.0 - posterior) * mu_irr * (1.0 - mu_irr))[:, None],
            ],
            axis=1,
        ).astype(BF16)
        grad_w = jnp.concatenate(
            [
                selector * (posterior * (click_float - mu_rel))[:, None],
                selector * ((1.0 - posterior) * (click_float - mu_irr))[:, None],
            ],
            axis=1,
        )
        feats = features.shape[1]
        grad_part = jnp.dot(features_t, grad_w, precision=lax.Precision.HIGHEST)
        stats_keep, stats_send = stats_blocks(core, features_t, hess_w, grad_part)

    with jax.named_scope("deep_grad"):
        slopes = pre_grad_b.reshape(part, n_mp, width).transpose(1, 0, 2)
        deep_part = jnp.stack(
            [
                lax.dot_general(
                    crossed_mine,
                    block_ahead(slopes, n_mp - mine, k),
                    (((0,), (0,)), ((), ())),
                    preferred_element_type=F32,
                ).astype(BF16)
                for k in range(n_mp)
            ]
        ).reshape(n_mp, n_zx, 2, depth, width)
        deep_keep = by_core(core, deep_part[:, :, 0], deep_part[:, :, 1])
        deep_send = by_core(core, deep_part[:, :, 1], deep_part[:, :, 0])
        deep_pair = (deep_keep.astype(F32) + swap(deep_send).astype(F32)).astype(BF16)
        deep_pair, stats_send, crossed_back = lax.optimization_barrier(
            (deep_pair, stats_send, crossed_back)
        )
        deep_sum = lax.all_to_all(deep_pair, "mp", 0, 0, tiled=True)
    with jax.named_scope("stats_sum"):
        stats_pair = (stats_keep.astype(F32) + swap(stats_send).astype(F32)).astype(BF16)
        stats_pair = stats_pair.reshape(n_z, n_x, feats + 16, 2 * ctx_count)
        stats_x = scatter_ahead(
            [block_ahead(stats_pair, my_x, t, 1) for t in range(n_x)], "x"
        ).astype(BF16)
        deep_sum, stats_x = lax.optimization_barrier((deep_sum, stats_x))
        deep_sum = jnp.sum(deep_sum.astype(F32), axis=0).astype(BF16)

    with jax.named_scope("cross_grad"):
        cross_pre_grad = crossed_back * base_float
        cross_pre_b = cross_pre_grad.astype(BF16)
        cross_part = jnp.stack(
            [
                lax.dot_general(
                    base[t], cross_pre_b, (((0,), (0,)), ((), ())), preferred_element_type=F32
                ).astype(BF16)
                for t in range(n_mp)
            ]
        )
        cross_part = to_absolute(cross_part, mine).reshape(n_zx, 2, depth, width)
        vec_part = jnp.concatenate([jnp.sum(cross_pre_grad, axis=0)[None], extra_sum])
        cross_keep = by_core(core, cross_part[:, 0], cross_part[:, 1])
        cross_send = by_core(core, cross_part[:, 1], cross_part[:, 0])
        cross_pair = (cross_keep.astype(F32) + swap(cross_send).astype(F32)).astype(BF16)
        vec_pair = (vec_part + swap(vec_part)).astype(BF16)
    with jax.named_scope("grads_x"):
        message = jnp.concatenate(
            [
                cross_pair,
                deep_sum,
                jnp.broadcast_to(vec_pair[None], (n_zx, 3, width)),
                jnp.zeros((n_zx, 5, width), BF16),
            ],
            axis=1,
        ).reshape(n_z, n_x, 2 * depth + 8, width)
        grads_x = scatter_ahead(
            [block_ahead(message, my_x, t, 1) for t in range(n_x)], "x"
        ).astype(BF16)
    with jax.named_scope("sums_z"):
        got = lax.all_to_all(jnp.concatenate([grads_x, stats_x], axis=1), "z", 0, 0, tiled=True)
        got_sum = jnp.sum(got.astype(F32), axis=0)
        matrix_shards = got_sum[: 2 * depth]
        vec_sum = got_sum[2 * depth : 2 * depth + 3]
        stats_sum = got_sum[2 * depth + 8 :]

    with jax.named_scope("norm"):
        squares = jnp.sum(matrix_shards * matrix_shards) + jnp.where(
            lax.axis_index(DP) == 0, jnp.sum(vec_sum * vec_sum), 0.0
        )
        squares = jnp.broadcast_to(squares, (2 * n_x * n_mp, 128))
        squares = lax.all_to_all(squares, ("x", "c", "mp"), 0, 0, tiled=True)
        squares = jnp.broadcast_to(jnp.sum(squares, axis=0)[None], (n_z, 128))
        squares = jnp.sum(lax.all_to_all(squares, "z", 0, 0, tiled=True), axis=0)[0]
        norm_scale = 1.0 / jnp.sqrt(squares / (2 * full * full + 3 * full) + 1e-06)

    with jax.named_scope("outputs"):
        hess_out = stats_sum[:feats].T.reshape(2, ctx_count, 1, feats)
        stat_grad_out = stats_sum[feats].reshape(2, ctx_count, 1)

    return (
        hess_out,
        stat_grad_out,
        matrix_shards[:depth] * norm_scale,
        matrix_shards[depth:] * norm_scale,
        vec_sum[0] * norm_scale,
        vec_sum[1] * norm_scale,
        vec_sum[2] * norm_scale,
    )


def solution(mesh):
    devices = np.asarray(mesh.devices).reshape(8, 4, 2, 4)
    fine = Mesh(devices, ("z", "x", "c", "mp"))
    return jax.shard_map(
        shards,
        mesh=fine,
        in_specs=(
            P(DP, None),
            P(DP),
            P(DP),
            P(DP),
            P(DP),
            P(None, "mp"),
            P(DP, "mp"),
            P(DP, "mp"),
            P("mp"),
            P("mp"),
            P("mp"),
            P(),
            P(),
            P("mp", None),
            P("mp", None),
        ),
        out_specs=(
            P(None, "mp", DP, None),
            P(None, "mp", DP),
            P(DP, "mp"),
            P(DP, "mp"),
            P("mp"),
            P("mp"),
            P("mp"),
        ),
        check_vma=False,
    )
```

```python
import jax
import jax.numpy as jnp
import numpy as np
from jax import lax
from jax.experimental import pallas as pl
from jax.experimental.pallas import tpu as pltpu
from jax.sharding import Mesh, PartitionSpec as P

DP = ("z", "x", "c")
BF16 = jnp.bfloat16
F32 = jnp.float32


def posterior_of(relevance, mu_rel, mu_irr, click_float):
    on_click = mu_rel * relevance / (mu_rel * relevance + mu_irr * (1.0 - relevance))
    no_click = (
        (1.0 - mu_rel)
        * relevance
        / ((1.0 - mu_rel) * relevance + (1.0 - mu_irr) * (1.0 - relevance))
    )
    return jnp.where(click_float > 0.5, on_click, no_click)


def table_lookup(indices, table):
    onehot_rows = (indices[:, None] == jnp.arange(table.shape[0])[None, :]).astype(F32)
    return jnp.dot(onehot_rows, table, precision=lax.Precision.HIGHEST)


def embed_kernel(ids_ref, table_ref, out_ref, wide_ref):
    rows, slots = ids_ref.shape
    vocab, width = table_ref.shape
    lanes = 256
    tile = 256
    ids = ids_ref[...]
    for s in range(slots):
        wide_ref[s] = jnp.broadcast_to(ids[:, s : s + 1], (rows, lanes)).astype(jnp.int16)
    lane = lax.broadcasted_iota(jnp.int32, (tile, lanes), 1)

    def body(r, carry):
        first = pl.multiple_of(r * tile, tile)
        total = jnp.zeros((tile, width), F32)
        for k in range(vocab // lanes):
            names = (lane + k * lanes).astype(jnp.int16)
            counts = jnp.zeros((tile, lanes), BF16)
            for s in range(slots):
                hit = wide_ref[s, pl.ds(first, tile), :] == names
                counts = counts + jnp.where(hit, jnp.ones((), BF16), jnp.zeros((), BF16))
            total = total + jnp.dot(
                counts, table_ref[k * lanes : (k + 1) * lanes, :], preferred_element_type=F32
            )
        out_ref[pl.ds(first, tile), :] = total.astype(BF16)
        return carry

    lax.fori_loop(0, rows // tile, body, 0)


def embed(ids, table):
    rows = ids.shape[0]
    return pl.pallas_call(
        embed_kernel,
        out_shape=jax.ShapeDtypeStruct((rows, table.shape[1]), BF16),
        in_specs=[pl.BlockSpec(memory_space=pltpu.VMEM)] * 2,
        out_specs=pl.BlockSpec(memory_space=pltpu.VMEM),
        scratch_shapes=[pltpu.VMEM((ids.shape[1], rows, 256), jnp.int16)],
        compiler_params=pltpu.CompilerParams(vmem_limit_bytes=40 * 2**20),
    )(ids, table)


def stats_kernel(core_ref, feats_ref, weights_ref, grads_ref, keep_ref, send_ref):
    feats = feats_ref.shape[0]
    group = 4
    core = core_ref[0]
    head = lax.broadcasted_iota(jnp.int32, (16, grads_ref.shape[1]), 0) == 0
    for out_ref, side in ((keep_ref, core), (send_ref, 1 - core)):

        def body(g, carry, out_ref=out_ref, side=side):
            features = feats_ref[...]
            places = [2 * (group * g + q) + side for q in range(group)]
            outer = jnp.concatenate(
                [(features * feats_ref[pl.ds(i, 1), :]).astype(BF16) for i in places]
            )
            sums = jnp.dot(outer, weights_ref[...], preferred_element_type=F32)
            for q in range(group):
                out_ref[group * g + q, 0:feats, :] = sums[q * feats : (q + 1) * feats].astype(BF16)
                row = jnp.where(head, grads_ref[pl.ds(places[q], 1), :], 0.0)
                out_ref[group * g + q, feats : feats + 16, :] = row.astype(BF16)
            return carry

        lax.fori_loop(0, feats // (2 * group), body, 0)


def stats_blocks(core, features_t, hess_w, grad_part):
    feats, columns = grad_part.shape
    shape = jax.ShapeDtypeStruct((feats // 2, feats + 16, columns), BF16)
    vmem = pl.BlockSpec(memory_space=pltpu.VMEM)
    return pl.pallas_call(
        stats_kernel,
        out_shape=(shape, shape),
        in_specs=[pl.BlockSpec(memory_space=pltpu.SMEM), vmem, vmem, vmem],
        out_specs=(vmem, vmem),
        compiler_params=pltpu.CompilerParams(vmem_limit_bytes=32 * 2**20),
        cost_estimate=pl.CostEstimate(flops=1000, transcendentals=0, bytes_accessed=1000),
    )(core.reshape(1).astype(jnp.int32), features_t, hess_w, grad_part)


def swap(value):
    return lax.ppermute(value, "c", [(0, 1), (1, 0)])


def gather(value, axes, count):
    wide = jnp.broadcast_to(value[None], (count,) + value.shape)
    return lax.all_to_all(wide, axes, 0, 0, tiled=True)


def shift(value, axis, count, ahead):
    return lax.ppermute(value, axis, [(i, (i + ahead) % count) for i in range(count)])


def gather_ahead(value, axis, count):
    return [value] + [shift(value, axis, count, count - t) for t in range(1, count)]


def scatter_ahead(parts, axis):
    count = len(parts)
    total = parts[0].astype(F32)
    for arrived in [shift(parts[t], axis, count, t) for t in range(1, count)]:
        total = total + arrived.astype(F32)
    return total


def to_absolute(blocks, mine):
    count = blocks.shape[0]
    return lax.dynamic_slice_in_dim(
        jnp.concatenate([blocks, blocks]), (count - mine) % count, count, 0
    )


def to_ahead(blocks, mine):
    return lax.dynamic_slice_in_dim(jnp.concatenate([blocks, blocks]), mine, blocks.shape[0], 0)


def block_ahead(blocks, mine, t, dim=0):
    count = blocks.shape[dim]
    return lax.dynamic_index_in_dim(blocks, (mine + t) % count, dim, keepdims=False)


def after(value, *earlier):
    return lax.optimization_barrier((value,) + earlier)[0]


def split3(value):
    high = lax.reduce_precision(value, 8, 7)
    rest = value - high
    middle = lax.reduce_precision(rest, 8, 7)
    return jnp.concatenate([high, middle, rest - middle], axis=-2).astype(BF16)


def join3(value):
    high, middle, low = jnp.split(value.astype(F32), 3, axis=-2)
    return high + (middle + low)


def by_core(core, even, odd):
    return jnp.where(core == 0, even, odd)


def shards(
    feature_ids,
    context_ids,
    shown_positions,
    clicked_positions,
    clicks,
    embed_table,
    cross_weight,
    deep_weight,
    cross_bias,
    deep_bias,
    out_weight,
    shown_embed,
    click_embed,
    theta_relevant,
    theta_irrelevant,
):
    n_z, n_x, n_mp = lax.axis_size("z"), lax.axis_size("x"), lax.axis_size("mp")
    n_zx = n_z * n_x
    n_dp = 2 * n_zx
    row_count = context_ids.shape[0]
    part = row_count // n_mp
    depth, width = cross_weight.shape
    full = n_mp * width
    half = full // 2
    core = lax.axis_index("c")
    mine = lax.axis_index("mp")

    my_x = lax.axis_index("x")

    with jax.named_scope("weights_dp"):
        held = gather(jnp.concatenate([cross_weight, deep_weight]), DP, n_dp)
        cross_col = held[:, :depth].reshape(full, width)
        deep_col = held[:, depth:].reshape(full, width)
    with jax.named_scope("embed"):
        base_rows = embed(feature_ids, embed_table)
        base_float = base_rows.astype(F32)
    with jax.named_scope("base_mp"):
        base = gather_ahead(base_rows, "mp", n_mp)

    with jax.named_scope("click_models"):
        context_ids = after(context_ids, held)
        shown_positions = after(shown_positions, held)
        clicked_positions = after(clicked_positions, held)
        ctx_count = theta_relevant.shape[0]
        local_ctx = context_ids - mine * ctx_count
        select = local_ctx[:, None] == jnp.arange(ctx_count)[None, :]
        selector = select.astype(F32)
        owned = (local_ctx >= 0) & (local_ctx < ctx_count)
        features = jnp.tanh(
            table_lookup(shown_positions, shown_embed)
            + table_lookup(clicked_positions, click_embed)
        )
        rel_rows = jnp.dot(selector, theta_relevant, precision=lax.Precision.HIGHEST)
        irr_rows = jnp.dot(selector, theta_irrelevant, precision=lax.Precision.HIGHEST)
        mu_rel = jax.nn.sigmoid(jnp.sum(rel_rows * features, axis=1))
        mu_irr = jax.nn.sigmoid(jnp.sum(irr_rows * features, axis=1))
        click_float = clicks.astype(F32)
        features_t = features.T
        click_mine = lax.dynamic_slice(click_float, (mine * part,), (part,))
    with jax.named_scope("vectors"):
        sent = jnp.where(owned[None, :], jnp.stack([mu_rel, mu_irr]), 0.0)
        sent = sent.reshape(2, n_mp, part).transpose(1, 0, 2)
        vectors = jnp.broadcast_to(jnp.stack([deep_bias, out_weight])[None], (n_mp, 2, width))
        vectors = split3(jnp.concatenate([sent, vectors], axis=1))
        vectors = jnp.concatenate([vectors, jnp.zeros((n_mp, 4, width), BF16)], axis=1)
        vectors = lax.optimization_barrier(vectors)

    with jax.named_scope("deep_weight_mp"):
        deep_half = lax.dynamic_slice(deep_col, (core * half, 0), (half, width))
        deep_half = gather_ahead(deep_half, "mp", n_mp)

    with jax.named_scope("cross"):
        cross_pre = cross_bias
        for t in range(n_mp):
            rows_t = lax.dynamic_slice(
                cross_col, (((mine + t) % n_mp) * width, 0), (width, width)
            )
            cross_pre = cross_pre + jnp.dot(base[t], rows_t, preferred_element_type=F32)
        crossed = (base_float * cross_pre + base_float).astype(BF16)
    with jax.named_scope("crossed_mp"):
        arrived = jnp.concatenate([crossed.reshape(n_mp, part, width), vectors], axis=1)
        arrived = lax.all_to_all(arrived, "mp", 0, 0, tiled=True)
        crossed_mine = arrived[:, :part].transpose(1, 0, 2).reshape(part, full)
        vectors = join3(arrived[:, part : part + 12])
        mu_mine = jnp.sum(vectors[:, :2], axis=0)
        vectors = to_ahead(vectors, mine)
        deep_bias_full = vectors[:, 2].reshape(full)
        out_full = vectors[:, 3].reshape(full)
    with jax.named_scope("deep_weight_core"):
        deep_half = lax.optimization_barrier((crossed, *deep_half))[1:]
        deep_half = jnp.concatenate(deep_half, axis=1)
        deep_other = swap(deep_half)
        deep_top = by_core(core, deep_half, deep_other)
        deep_low = by_core(core, deep_other, deep_half)
    with jax.named_scope("deep"):
        deep_pre = (
            jnp.dot(crossed_mine[:, :half], deep_top, preferred_element_type=F32)
            + jnp.dot(crossed_mine[:, half:], deep_low, preferred_element_type=F32)
            + deep_bias_full
        )
        gating = jax.nn.sigmoid(deep_pre)
        hidden = (deep_pre * gating).astype(BF16).astype(F32)
        slope = gating * (1.0 + deep_pre * (1.0 - gating))
        score = jnp.sum(hidden * out_full, axis=1)
        rel_mine = jax.nn.sigmoid(score)
        post_mine = posterior_of(rel_mine, mu_mine[0], mu_mine[1], click_mine)
        score_grad = rel_mine - post_mine
        pre_grad = score_grad[:, None] * out_full[None, :] * slope
        pre_grad_b = pre_grad.astype(BF16)
        deep_bias_part = jnp.sum(pre_grad, axis=0)
        out_part = jnp.sum(score_grad[:, None] * hidden, axis=0)
    with jax.named_scope("crossed_grad"):
        back = []
        for k in range(n_mp):
            rows = deep_top if k * width < half else deep_low
            first = (k * width) % half
            back.append(
                lax.dot_general(
                    pre_grad_b,
                    rows[first : first + width],
                    (((1,), (1,)), ((), ())),
                    preferred_element_type=F32,
                ).astype(BF16)
            )
        back = jnp.stack(back)
        extra = jnp.stack([deep_bias_part, out_part]).reshape(2, n_mp, width).transpose(1, 0, 2)
        extra = to_absolute(extra, mine)
        tail = jnp.concatenate([split3(extra), jnp.zeros((n_mp, 2, width), BF16)], axis=1)
        tail = lax.optimization_barrier(tail)
        back = jnp.concatenate([back, tail], axis=1)
        rel_sent = after(rel_mine, back)
        back = lax.all_to_all(back, "mp", 0, 0, tiled=True)
        crossed_back = back[:, :part].reshape(row_count, width).astype(F32)
        extra_sum = jnp.sum(join3(back[:, part : part + 6]), axis=0)
    with jax.named_scope("stats"):
        relevance = jnp.stack(gather_ahead(rel_sent, "mp", n_mp))
        relevance = to_absolute(relevance, mine).reshape(row_count)
        posterior = posterior_of(relevance, mu_rel, mu_irr, click_float)
        hess_w = jnp.concatenate(
            [
                selector * (posterior * mu_rel * (1.0 - mu_rel))[:, None],
                selector * ((1.0 - posterior) * mu_irr * (1.0 - mu_irr))[:, None],
            ],
            axis=1,
        ).astype(BF16)
        grad_w = jnp.concatenate(
            [
                selector * (posterior * (click_float - mu_rel))[:, None],
                selector * ((1.0 - posterior) * (click_float - mu_irr))[:, None],
            ],
            axis=1,
        )
        feats = features.shape[1]
        grad_part = jnp.dot(features_t, grad_w, precision=lax.Precision.HIGHEST)
        stats_keep, stats_send = stats_blocks(core, features_t, hess_w, grad_part)

    with jax.named_scope("deep_grad"):
        slopes = pre_grad_b.reshape(part, n_mp, width).transpose(1, 0, 2)
        deep_part = jnp.stack(
            [
                lax.dot_general(
                    crossed_mine,
                    block_ahead(slopes, n_mp - mine, k),
                    (((0,), (0,)), ((), ())),
                    preferred_element_type=F32,
                ).astype(BF16)
                for k in range(n_mp)
            ]
        ).reshape(n_mp, n_zx, 2, depth, width)
        deep_keep = by_core(core, deep_part[:, :, 0], deep_part[:, :, 1])
        deep_send = by_core(core, deep_part[:, :, 1], deep_part[:, :, 0])
        deep_pair = (deep_keep.astype(F32) + swap(deep_send).astype(F32)).astype(BF16)
        deep_sum = lax.all_to_all(deep_pair, "mp", 0, 0, tiled=True)
    with jax.named_scope("stats_sum"):
        stats_pair = (stats_keep.astype(F32) + swap(stats_send).astype(F32)).astype(BF16)
        stats_pair = stats_pair[:, : feats + 8].reshape(n_z, n_x, feats + 8, 2 * ctx_count)
        crossed_back = after(crossed_back, stats_pair, deep_pair)
        stats_parts = [block_ahead(stats_pair, my_x, t, 1) for t in range(n_x)]
        stats_parts = stats_parts[:1] + [
            shift(stats_parts[t], "x", n_x, t) for t in range(1, n_x)
        ]
        deep_sum, stats_parts[1], stats_parts[-1] = lax.optimization_barrier(
            (deep_sum, stats_parts[1], stats_parts[-1])
        )
        deep_sum = jnp.sum(deep_sum.astype(F32), axis=0).astype(BF16)

    with jax.named_scope("cross_grad"):
        cross_pre_grad = crossed_back * base_float
        cross_pre_b = cross_pre_grad.astype(BF16)
        cross_part = jnp.stack(
            [
                lax.dot_general(
                    base[t], cross_pre_b, (((0,), (0,)), ((), ())), preferred_element_type=F32
                ).astype(BF16)
                for t in range(n_mp)
            ]
        )
        cross_part = to_absolute(cross_part, mine).reshape(n_zx, 2, depth, width)
        vec_part = jnp.concatenate([jnp.sum(cross_pre_grad, axis=0)[None], extra_sum])
        cross_keep = by_core(core, cross_part[:, 0], cross_part[:, 1])
        cross_send = by_core(core, cross_part[:, 1], cross_part[:, 0])
        cross_pair = (cross_keep.astype(F32) + swap(cross_send).astype(F32)).astype(BF16)
        vec_pair = (vec_part + swap(vec_part)).astype(BF16)
    with jax.named_scope("grads_x"):
        message = jnp.concatenate(
            [
                cross_pair,
                deep_sum,
                jnp.broadcast_to(vec_pair[None], (n_zx, 3, width)),
                jnp.zeros((n_zx, 5, width), BF16),
            ],
            axis=1,
        ).reshape(n_z, n_x, 2 * depth + 8, width)
        grads_x = scatter_ahead(
            [block_ahead(message, my_x, t, 1) for t in range(n_x)], "x"
        ).astype(BF16)
    with jax.named_scope("sums_z"):
        stats_x = sum(p.astype(F32) for p in stats_parts).astype(BF16)
        got = lax.all_to_all(jnp.concatenate([grads_x, stats_x], axis=1), "z", 0, 0, tiled=True)
        got_sum = jnp.sum(got.astype(F32), axis=0)
        matrix_shards = got_sum[: 2 * depth]
        vec_sum = got_sum[2 * depth : 2 * depth + 3]
        stats_sum = got_sum[2 * depth + 8 :]

    with jax.named_scope("norm"):
        squares = jnp.sum(matrix_shards * matrix_shards) + jnp.where(
            lax.axis_index(DP) == 0, jnp.sum(vec_sum * vec_sum), 0.0
        )
        squares = jnp.broadcast_to(squares, (2 * n_x * n_mp, 128))
        squares = lax.all_to_all(squares, ("x", "c", "mp"), 0, 0, tiled=True)
        squares = jnp.broadcast_to(jnp.sum(squares, axis=0)[None], (n_z, 128))
        squares = jnp.sum(lax.all_to_all(squares, "z", 0, 0, tiled=True), axis=0)[0]
        norm_scale = 1.0 / jnp.sqrt(squares / (2 * full * full + 3 * full) + 1e-06)

    with jax.named_scope("outputs"):
        hess_out = stats_sum[:feats].T.reshape(2, ctx_count, 1, feats)
        stat_grad_out = stats_sum[feats].reshape(2, ctx_count, 1)

    return (
        hess_out,
        stat_grad_out,
        matrix_shards[:depth] * norm_scale,
        matrix_shards[depth:] * norm_scale,
        vec_sum[0] * norm_scale,
        vec_sum[1] * norm_scale,
        vec_sum[2] * norm_scale,
    )


def solution(mesh):
    devices = np.asarray(mesh.devices).reshape(8, 4, 2, 4)
    fine = Mesh(devices, ("z", "x", "c", "mp"))
    return jax.shard_map(
        shards,
        mesh=fine,
        in_specs=(
            P(DP, None),
            P(DP),
            P(DP),
            P(DP),
            P(DP),
            P(None, "mp"),
            P(DP, "mp"),
            P(DP, "mp"),
            P("mp"),
            P("mp"),
            P("mp"),
            P(),
            P(),
            P("mp", None),
            P("mp", None),
        ),
        out_specs=(
            P(None, "mp", DP, None),
            P(None, "mp", DP),
            P(DP, "mp"),
            P(DP, "mp"),
            P("mp"),
            P("mp"),
            P("mp"),
        ),
        check_vma=False,
    )
```

```python
import jax
import jax.numpy as jnp
import numpy as np
from jax import lax
from jax.experimental import pallas as pl
from jax.experimental.pallas import tpu as pltpu
from jax.sharding import Mesh, PartitionSpec as P

DP = ("z", "x", "c")
BF16 = jnp.bfloat16
F32 = jnp.float32


def posterior_of(relevance, mu_rel, mu_irr, click_float):
    on_click = mu_rel * relevance / (mu_rel * relevance + mu_irr * (1.0 - relevance))
    no_click = (
        (1.0 - mu_rel)
        * relevance
        / ((1.0 - mu_rel) * relevance + (1.0 - mu_irr) * (1.0 - relevance))
    )
    return jnp.where(click_float > 0.5, on_click, no_click)


def table_lookup(indices, table):
    onehot_rows = (indices[:, None] == jnp.arange(table.shape[0])[None, :]).astype(F32)
    return jnp.dot(onehot_rows, table, precision=lax.Precision.HIGHEST)


def embed_kernel(ids_ref, table_ref, out_ref, wide_ref):
    rows, slots = ids_ref.shape
    vocab, width = table_ref.shape
    lanes = 256
    tile = 256
    ids = ids_ref[...]
    for s in range(slots):
        wide_ref[s] = jnp.broadcast_to(ids[:, s : s + 1], (rows, lanes)).astype(jnp.int16)
    lane = lax.broadcasted_iota(jnp.int32, (tile, lanes), 1)

    def body(r, carry):
        first = pl.multiple_of(r * tile, tile)
        total = jnp.zeros((tile, width), F32)
        for k in range(vocab // lanes):
            names = (lane + k * lanes).astype(jnp.int16)
            counts = jnp.zeros((tile, lanes), BF16)
            for s in range(slots):
                hit = wide_ref[s, pl.ds(first, tile), :] == names
                counts = counts + jnp.where(hit, jnp.ones((), BF16), jnp.zeros((), BF16))
            total = total + jnp.dot(
                counts, table_ref[k * lanes : (k + 1) * lanes, :], preferred_element_type=F32
            )
        out_ref[pl.ds(first, tile), :] = total.astype(BF16)
        return carry

    lax.fori_loop(0, rows // tile, body, 0)


def embed(ids, table):
    rows = ids.shape[0]
    return pl.pallas_call(
        embed_kernel,
        out_shape=jax.ShapeDtypeStruct((rows, table.shape[1]), BF16),
        in_specs=[pl.BlockSpec(memory_space=pltpu.VMEM)] * 2,
        out_specs=pl.BlockSpec(memory_space=pltpu.VMEM),
        scratch_shapes=[pltpu.VMEM((ids.shape[1], rows, 256), jnp.int16)],
        compiler_params=pltpu.CompilerParams(vmem_limit_bytes=40 * 2**20),
    )(ids, table)


def stats_kernel(core_ref, feats_ref, weights_ref, grads_ref, keep_ref, send_ref):
    feats = feats_ref.shape[0]
    group = 4
    core = core_ref[0]
    head = lax.broadcasted_iota(jnp.int32, (16, grads_ref.shape[1]), 0) == 0
    for out_ref, side in ((keep_ref, core), (send_ref, 1 - core)):

        def body(g, carry, out_ref=out_ref, side=side):
            features = feats_ref[...]
            places = [2 * (group * g + q) + side for q in range(group)]
            outer = jnp.concatenate(
                [(features * feats_ref[pl.ds(i, 1), :]).astype(BF16) for i in places]
            )
            sums = jnp.dot(outer, weights_ref[...], preferred_element_type=F32)
            for q in range(group):
                out_ref[group * g + q, 0:feats, :] = sums[q * feats : (q + 1) * feats].astype(BF16)
                row = jnp.where(head, grads_ref[pl.ds(places[q], 1), :], 0.0)
                out_ref[group * g + q, feats : feats + 16, :] = row.astype(BF16)
            return carry

        lax.fori_loop(0, feats // (2 * group), body, 0)


def stats_blocks(core, features_t, hess_w, grad_part):
    feats, columns = grad_part.shape
    shape = jax.ShapeDtypeStruct((feats // 2, feats + 16, columns), BF16)
    vmem = pl.BlockSpec(memory_space=pltpu.VMEM)
    return pl.pallas_call(
        stats_kernel,
        out_shape=(shape, shape),
        in_specs=[pl.BlockSpec(memory_space=pltpu.SMEM), vmem, vmem, vmem],
        out_specs=(vmem, vmem),
        compiler_params=pltpu.CompilerParams(vmem_limit_bytes=32 * 2**20),
        cost_estimate=pl.CostEstimate(flops=1000, transcendentals=0, bytes_accessed=1000),
    )(core.reshape(1).astype(jnp.int32), features_t, hess_w, grad_part)


def swap(value):
    return lax.ppermute(value, "c", [(0, 1), (1, 0)])


def gather(value, axes, count):
    wide = jnp.broadcast_to(value[None], (count,) + value.shape)
    return lax.all_to_all(wide, axes, 0, 0, tiled=True)


def shift(value, axis, count, ahead):
    return lax.ppermute(value, axis, [(i, (i + ahead) % count) for i in range(count)])


def gather_ahead(value, axis, count):
    return [value] + [shift(value, axis, count, count - t) for t in range(1, count)]


def scatter_ahead(parts, axis):
    count = len(parts)
    total = parts[0].astype(F32)
    for arrived in [shift(parts[t], axis, count, t) for t in range(1, count)]:
        total = total + arrived.astype(F32)
    return total


def to_absolute(blocks, mine):
    count = blocks.shape[0]
    return lax.dynamic_slice_in_dim(
        jnp.concatenate([blocks, blocks]), (count - mine) % count, count, 0
    )


def to_ahead(blocks, mine):
    return lax.dynamic_slice_in_dim(jnp.concatenate([blocks, blocks]), mine, blocks.shape[0], 0)


def block_ahead(blocks, mine, t, dim=0):
    count = blocks.shape[dim]
    return lax.dynamic_index_in_dim(blocks, (mine + t) % count, dim, keepdims=False)


def after(value, *earlier):
    return lax.optimization_barrier((value,) + earlier)[0]


def split3(value):
    high = lax.reduce_precision(value, 8, 7)
    rest = value - high
    middle = lax.reduce_precision(rest, 8, 7)
    return jnp.concatenate([high, middle, rest - middle], axis=-2).astype(BF16)


def join3(value):
    high, middle, low = jnp.split(value.astype(F32), 3, axis=-2)
    return high + (middle + low)


def by_core(core, even, odd):
    return jnp.where(core == 0, even, odd)


def shards(
    feature_ids,
    context_ids,
    shown_positions,
    clicked_positions,
    clicks,
    embed_table,
    cross_weight,
    deep_weight,
    cross_bias,
    deep_bias,
    out_weight,
    shown_embed,
    click_embed,
    theta_relevant,
    theta_irrelevant,
):
    n_z, n_x, n_mp = lax.axis_size("z"), lax.axis_size("x"), lax.axis_size("mp")
    n_zx = n_z * n_x
    n_dp = 2 * n_zx
    row_count = context_ids.shape[0]
    part = row_count // n_mp
    depth, width = cross_weight.shape
    full = n_mp * width
    half = full // 2
    core = lax.axis_index("c")
    mine = lax.axis_index("mp")

    my_x = lax.axis_index("x")

    with jax.named_scope("weights_dp"):
        held = gather(jnp.concatenate([cross_weight, deep_weight]), DP, n_dp)
        cross_col = held[:, :depth].reshape(full, width)
        deep_col = held[:, depth:].reshape(full, width)
    with jax.named_scope("embed"):
        base_rows = embed(feature_ids, embed_table)
        base_float = base_rows.astype(F32)
    with jax.named_scope("base_mp"):
        base = gather_ahead(base_rows, "mp", n_mp)

    with jax.named_scope("click_models"):
        context_ids = after(context_ids, held)
        shown_positions = after(shown_positions, held)
        clicked_positions = after(clicked_positions, held)
        ctx_count = theta_relevant.shape[0]
        local_ctx = context_ids - mine * ctx_count
        select = local_ctx[:, None] == jnp.arange(ctx_count)[None, :]
        selector = select.astype(F32)
        owned = (local_ctx >= 0) & (local_ctx < ctx_count)
        features = jnp.tanh(
            table_lookup(shown_positions, shown_embed)
            + table_lookup(clicked_positions, click_embed)
        )
        rel_rows = jnp.dot(selector, theta_relevant, precision=lax.Precision.HIGHEST)
        irr_rows = jnp.dot(selector, theta_irrelevant, precision=lax.Precision.HIGHEST)
        mu_rel = jax.nn.sigmoid(jnp.sum(rel_rows * features, axis=1))
        mu_irr = jax.nn.sigmoid(jnp.sum(irr_rows * features, axis=1))
        click_float = clicks.astype(F32)
        features_t = features.T
        click_mine = lax.dynamic_slice(click_float, (mine * part,), (part,))
    with jax.named_scope("vectors"):
        sent = jnp.where(owned[None, :], jnp.stack([mu_rel, mu_irr]), 0.0)
        sent = sent.reshape(2, n_mp, part).transpose(1, 0, 2)
        vectors = jnp.broadcast_to(jnp.stack([deep_bias, out_weight])[None], (n_mp, 2, width))
        vectors = split3(jnp.concatenate([sent, vectors], axis=1))
        vectors = jnp.concatenate([vectors, jnp.zeros((n_mp, 4, width), BF16)], axis=1)
        vectors = lax.optimization_barrier(vectors)

    with jax.named_scope("deep_weight_mp"):
        deep_half = lax.dynamic_slice(deep_col, (core * half, 0), (half, width))
        deep_half = gather_ahead(deep_half, "mp", n_mp)

    with jax.named_scope("cross"):
        cross_pre = cross_bias
        for t in range(n_mp):
            rows_t = lax.dynamic_slice(
                cross_col, (((mine + t) % n_mp) * width, 0), (width, width)
            )
            cross_pre = cross_pre + jnp.dot(base[t], rows_t, preferred_element_type=F32)
        crossed = (base_float * cross_pre + base_float).astype(BF16)
    with jax.named_scope("crossed_mp"):
        arrived = jnp.concatenate([crossed.reshape(n_mp, part, width), vectors], axis=1)
        arrived = lax.all_to_all(arrived, "mp", 0, 0, tiled=True)
        crossed_mine = arrived[:, :part].transpose(1, 0, 2).reshape(part, full)
        vectors = join3(arrived[:, part : part + 12])
        mu_mine = jnp.sum(vectors[:, :2], axis=0)
        vectors = to_ahead(vectors, mine)
        deep_bias_full = vectors[:, 2].reshape(full)
        out_full = vectors[:, 3].reshape(full)
    with jax.named_scope("deep_weight_core"):
        deep_half = lax.optimization_barrier((crossed, *deep_half))[1:]
        deep_half = jnp.concatenate(deep_half, axis=1)
        deep_other = swap(deep_half)
        deep_top = by_core(core, deep_half, deep_other)
        deep_low = by_core(core, deep_other, deep_half)
    with jax.named_scope("deep"):
        deep_pre = (
            jnp.dot(crossed_mine[:, :half], deep_top, preferred_element_type=F32)
            + jnp.dot(crossed_mine[:, half:], deep_low, preferred_element_type=F32)
            + deep_bias_full
        )
        gating = jax.nn.sigmoid(deep_pre)
        hidden = (deep_pre * gating).astype(BF16).astype(F32)
        slope = gating * (1.0 + deep_pre * (1.0 - gating))
        score = jnp.sum(hidden * out_full, axis=1)
        rel_mine = jax.nn.sigmoid(score)
        post_mine = posterior_of(rel_mine, mu_mine[0], mu_mine[1], click_mine)
        score_grad = rel_mine - post_mine
        pre_grad = score_grad[:, None] * out_full[None, :] * slope
        pre_grad_b = pre_grad.astype(BF16)
        deep_bias_part = jnp.sum(pre_grad, axis=0)
        out_part = jnp.sum(score_grad[:, None] * hidden, axis=0)
    with jax.named_scope("crossed_grad"):
        back = []
        for k in range(n_mp):
            rows = deep_top if k * width < half else deep_low
            first = (k * width) % half
            back.append(
                lax.dot_general(
                    pre_grad_b,
                    rows[first : first + width],
                    (((1,), (1,)), ((), ())),
                    preferred_element_type=F32,
                ).astype(BF16)
            )
        back = jnp.stack(back)
        extra = jnp.stack([deep_bias_part, out_part]).reshape(2, n_mp, width).transpose(1, 0, 2)
        extra = to_absolute(extra, mine)
        tail = jnp.concatenate([split3(extra), jnp.zeros((n_mp, 2, width), BF16)], axis=1)
        tail = lax.optimization_barrier(tail)
        back = jnp.concatenate([back, tail], axis=1)
        rel_sent = after(rel_mine, back)
        back = lax.all_to_all(back, "mp", 0, 0, tiled=True)
        crossed_back = back[:, :part].reshape(row_count, width).astype(F32)
        extra_sum = jnp.sum(join3(back[:, part : part + 6]), axis=0)
    with jax.named_scope("stats"):
        relevance = jnp.stack(gather_ahead(rel_sent, "mp", n_mp))
        relevance = to_absolute(relevance, mine).reshape(row_count)
        posterior = posterior_of(relevance, mu_rel, mu_irr, click_float)
        hess_w = jnp.concatenate(
            [
                selector * (posterior * mu_rel * (1.0 - mu_rel))[:, None],
                selector * ((1.0 - posterior) * mu_irr * (1.0 - mu_irr))[:, None],
            ],
            axis=1,
        ).astype(BF16)
        grad_w = jnp.concatenate(
            [
                selector * (posterior * (click_float - mu_rel))[:, None],
                selector * ((1.0 - posterior) * (click_float - mu_irr))[:, None],
            ],
            axis=1,
        )
        feats = features.shape[1]
        grad_part = jnp.dot(features_t, grad_w, precision=lax.Precision.HIGHEST)
        stats_keep, stats_send = stats_blocks(core, features_t, hess_w, grad_part)

    with jax.named_scope("deep_grad"):
        slopes = pre_grad_b.reshape(part, n_mp, width).transpose(1, 0, 2)
        deep_part = jnp.stack(
            [
                lax.dot_general(
                    crossed_mine,
                    block_ahead(slopes, n_mp - mine, k),
                    (((0,), (0,)), ((), ())),
                    preferred_element_type=F32,
                ).astype(BF16)
                for k in range(n_mp)
            ]
        ).reshape(n_mp, n_zx, 2, depth, width)
        deep_keep = by_core(core, deep_part[:, :, 0], deep_part[:, :, 1])
        deep_send = by_core(core, deep_part[:, :, 1], deep_part[:, :, 0])
        deep_pair = (deep_keep.astype(F32) + swap(deep_send).astype(F32)).astype(BF16)
        deep_sum = lax.all_to_all(deep_pair, "mp", 0, 0, tiled=True)
    with jax.named_scope("stats_sum"):
        stats_pair = (stats_keep.astype(F32) + swap(stats_send).astype(F32)).astype(BF16)
        stats_pair = stats_pair[:, : feats + 8].reshape(n_z, n_x, feats + 8, 2 * ctx_count)
        crossed_back = after(crossed_back, stats_pair, deep_pair)
        stats_parts = [block_ahead(stats_pair, my_x, t, 1) for t in range(n_x)]
        stats_parts[1] = shift(stats_parts[1], "x", n_x, 1)
        stats_parts[-1] = shift(stats_parts[-1], "x", n_x, n_x - 1)
        deep_sum, stats_parts[1], stats_parts[-1] = lax.optimization_barrier(
            (deep_sum, stats_parts[1], stats_parts[-1])
        )
        for t in range(2, n_x - 1):
            stats_parts[t] = shift(after(stats_parts[t], deep_sum), "x", n_x, t)
        deep_sum = jnp.sum(deep_sum.astype(F32), axis=0).astype(BF16)

    with jax.named_scope("cross_grad"):
        cross_pre_grad = crossed_back * base_float
        cross_pre_b = cross_pre_grad.astype(BF16)
        cross_part = jnp.stack(
            [
                lax.dot_general(
                    base[t], cross_pre_b, (((0,), (0,)), ((), ())), preferred_element_type=F32
                ).astype(BF16)
                for t in range(n_mp)
            ]
        )
        cross_part = to_absolute(cross_part, mine).reshape(n_zx, 2, depth, width)
        vec_part = jnp.concatenate([jnp.sum(cross_pre_grad, axis=0)[None], extra_sum])
        cross_keep = by_core(core, cross_part[:, 0], cross_part[:, 1])
        cross_send = by_core(core, cross_part[:, 1], cross_part[:, 0])
        cross_pair = (cross_keep.astype(F32) + swap(cross_send).astype(F32)).astype(BF16)
        vec_pair = (vec_part + swap(vec_part)).astype(BF16)
    with jax.named_scope("grads_x"):
        message = jnp.concatenate(
            [
                cross_pair,
                deep_sum,
                jnp.broadcast_to(vec_pair[None], (n_zx, 3, width)),
                jnp.zeros((n_zx, 5, width), BF16),
            ],
            axis=1,
        ).reshape(n_z, n_x, 2 * depth + 8, width)
        grads_x = scatter_ahead(
            [block_ahead(message, my_x, t, 1) for t in range(n_x)], "x"
        ).astype(BF16)
    with jax.named_scope("sums_z"):
        stats_x = sum(p.astype(F32) for p in stats_parts).astype(BF16)
        got = lax.all_to_all(jnp.concatenate([grads_x, stats_x], axis=1), "z", 0, 0, tiled=True)
        got_sum = jnp.sum(got.astype(F32), axis=0)
        matrix_shards = got_sum[: 2 * depth]
        vec_sum = got_sum[2 * depth : 2 * depth + 3]
        stats_sum = got_sum[2 * depth + 8 :]

    with jax.named_scope("norm"):
        squares = jnp.sum(matrix_shards * matrix_shards) + jnp.where(
            lax.axis_index(DP) == 0, jnp.sum(vec_sum * vec_sum), 0.0
        )
        squares = jnp.broadcast_to(squares, (2 * n_x * n_mp, 128))
        squares = lax.all_to_all(squares, ("x", "c", "mp"), 0, 0, tiled=True)
        squares = jnp.broadcast_to(jnp.sum(squares, axis=0)[None], (n_z, 128))
        squares = jnp.sum(lax.all_to_all(squares, "z", 0, 0, tiled=True), axis=0)[0]
        norm_scale = 1.0 / jnp.sqrt(squares / (2 * full * full + 3 * full) + 1e-06)

    with jax.named_scope("outputs"):
        hess_out = stats_sum[:feats].T.reshape(2, ctx_count, 1, feats)
        stat_grad_out = stats_sum[feats].reshape(2, ctx_count, 1)

    return (
        hess_out,
        stat_grad_out,
        matrix_shards[:depth] * norm_scale,
        matrix_shards[depth:] * norm_scale,
        vec_sum[0] * norm_scale,
        vec_sum[1] * norm_scale,
        vec_sum[2] * norm_scale,
    )


def solution(mesh):
    devices = np.asarray(mesh.devices).reshape(8, 4, 2, 4)
    fine = Mesh(devices, ("z", "x", "c", "mp"))
    return jax.shard_map(
        shards,
        mesh=fine,
        in_specs=(
            P(DP, None),
            P(DP),
            P(DP),
            P(DP),
            P(DP),
            P(None, "mp"),
            P(DP, "mp"),
            P(DP, "mp"),
            P("mp"),
            P("mp"),
            P("mp"),
            P(),
            P(),
            P("mp", None),
            P("mp", None),
        ),
        out_specs=(
            P(None, "mp", DP, None),
            P(None, "mp", DP),
            P(DP, "mp"),
            P(DP, "mp"),
            P("mp"),
            P("mp"),
            P("mp"),
        ),
        check_vma=False,
    )
```
